128 devices in a mesh: grp: 4 (over y_lo, core), blk: 32 (over z, y_hi, x).
Axes of the slice: x: 4, y: 4 (y_hi: 2, y_lo: 2; y = y_hi * 2 + y_lo), z: 4, core: 2. Of those that a mesh axis runs over, the one named last changes fastest.
Arguments:
- unlabeled: bfloat16 [65536, 1024], P('blk'), may hold values from -10 to 10
- labeled: bfloat16 [131072, 1024], P(('grp', 'blk')), may hold values from -5 to 5
- picks: int32 [128], replicated, may hold values from 0 to 65535, as said below
Outputs:
- nearest: float32 [65536], P('blk')
The draws below stay inside these ranges and needn't reach their ends.
Inputs may be any that keep to these rules, and one draw needn't show every extreme that they name: `picks`: indices may repeat; row 0 and row 65535 are always among them.
All inputs are finite; a program needn't handle non-finite values.
Results may differ from the reference program's by a relative error of at most 0.0003.
Values may be sent and summed in bfloat16 or wider, within the bound.
A program may use at most 64 MiB of HBM per device.

```python
import jax
import jax.numpy as jnp
from jax import lax

D = 1024
U_DEV = 2048
L_DEV = 1024
STEPS = 2
PICKS = 128
UN = 65536
N_GRP = 4
N_BLK = 32


def labeled_row(base, index):
    sub = jax.random.fold_in(base, index)
    return jax.random.truncated_normal(sub, -5.0, 5.0, (D,), jnp.float32)


def pick_indices(key):
    sub = jax.random.fold_in(key, 37)
    key_raw, key_slot = jax.random.split(sub, 2)
    count = N_BLK * U_DEV
    raw = jax.random.randint(key_raw, (PICKS,), 0, count, jnp.int32)
    slots = jax.random.permutation(key_slot, PICKS)[:2]
    raw = raw.at[slots[0]].set(0)
    raw = raw.at[slots[1]].set(count - 1)
    return raw.astype(jnp.int32)


def unit_noise(sub, shape):
    return jax.random.truncated_normal(sub, -5.0, 5.0, shape, jnp.float32)


def draw_picks(key, part):
    return pick_indices(key)


def draw_labeled(key, part):
    base = jax.random.fold_in(key, 11)
    count = N_GRP * N_BLK * L_DEV
    indices = jnp.arange(count, dtype=jnp.int32)
    rows = jax.vmap(lambda index: labeled_row(base, index))(indices)
    return rows.astype(jnp.bfloat16)


def draw_unlabeled(key, part):
    base = jax.random.fold_in(key, 11)
    mixer = jax.random.fold_in(key, 23)
    keys = jax.random.split(mixer, 9)
    key_group, key_back, key_row, key_weight, key_noise = (keys[0], keys[1], keys[2], keys[3], keys[4])
    key_coin, key_target, key_close, key_near = (keys[5], keys[6], keys[7], keys[8])
    count = N_BLK * U_DEV
    indices = jnp.arange(count, dtype=jnp.int32)
    owner = indices // U_DEV
    group = jax.random.randint(key_group, (count,), 0, N_GRP, jnp.int32)
    back = jax.random.randint(key_back, (count,), 0, STEPS + 1, jnp.int32)
    within = jax.random.randint(key_row, (count,), 0, L_DEV, jnp.int32)
    source = (group * N_BLK + (owner - back) % N_BLK) * L_DEV + within
    partner = jax.vmap(lambda index: labeled_row(base, index))(source)
    weight = jax.random.uniform(key_weight, (count, 1), jnp.float32, 0.3, 0.9)
    noise = unit_noise(key_noise, (count, D))
    drawn = weight * partner + jnp.sqrt(1.0 - weight * weight) * noise
    picks = pick_indices(key)
    picked = jnp.any(indices[:, None] == picks[None, :], axis=1)
    coin = jax.random.randint(key_coin, (count,), 0, 4, jnp.int32)
    variant = (coin == 0) & jnp.logical_not(picked)
    target = picks[jax.random.randint(key_target, (count,), 0, PICKS, jnp.int32)]
    close = jax.random.uniform(key_close, (count, 1), jnp.float32, 0.9, 0.97)
    near_noise = unit_noise(key_near, (count, D))
    near = close * drawn[target] + jnp.sqrt(1.0 - close * close) * near_noise
    rows = jnp.where(variant[:, None], near, drawn)
    return rows.astype(jnp.bfloat16)


def setup_inputs(seed: int = 0) -> dict:
    seeds = jax.random.split(jax.random.key(seed), 4)
    unlabeled = draw_unlabeled(jax.random.fold_in(seeds[3], 71), 0)
    labeled = draw_labeled(jax.random.fold_in(seeds[3], 71), 0)
    picks = draw_picks(jax.random.fold_in(seeds[3], 71), 0)
    return dict(unlabeled=unlabeled, labeled=labeled, picks=picks)


def squares(rows):
    wide = rows.astype(jnp.float32)
    return jnp.sum(wide * wide, axis=1)


def least(rows, rows_sq, others):
    others_sq = squares(others)
    inner = jnp.dot(rows, others.T, preferred_element_type=jnp.float32)
    scaled = (rows_sq[:, None] + others_sq[None, :] - 2.0 * inner) / D
    return jnp.min(scaled, axis=1)


def reference(unlabeled, labeled, picks):
    blocks = labeled.reshape(N_GRP, N_BLK, L_DEV, D)
    rows = unlabeled.reshape(N_BLK, U_DEV, D)

    def per_block(index):
        mine = lax.dynamic_index_in_dim(rows, index, 0, keepdims=False)
        mine_sq = squares(mine)
        best = jnp.full((U_DEV,), jnp.inf, jnp.float32)
        for back in range(STEPS + 1):
            source = ((index - back) % N_BLK).astype(jnp.int32)
            pool = lax.dynamic_index_in_dim(blocks, source, 1, keepdims=False)
            for group in range(N_GRP):
                best = jnp.minimum(best, least(mine, mine_sq, pool[group]))
        return best

    labeled_min = lax.map(per_block, jnp.arange(N_BLK, dtype=jnp.int32)).reshape(UN)
    pick_rows = unlabeled[picks]
    pick_min = least(unlabeled, squares(unlabeled), pick_rows)
    return jnp.minimum(labeled_min, pick_min)
```

```python
import jax
import jax.numpy as jnp
from jax import lax
from jax.experimental import pallas as pl
from jax.experimental.pallas import tpu as pltpu
from jax.sharding import PartitionSpec as P

MESH = pl.DeviceIdType.MESH
F32 = jnp.float32
BF16 = jnp.bfloat16

D = 1024
HALF = 1024
T1 = 256
T2 = 128
TC = 128
Q = 64
NM = (T1 + TC) // Q
NP = (T2 + TC) // Q
NT1 = T1 // Q
NT2 = T2 // Q
PK = 32
LT = 512
COLS = 256


def minus_off(role, i):
    if i < NT1:
        return role * T1 + i * Q
    return 2 * T1 + 2 * T2 + role * TC + (i - NT1) * Q


def plus_off(role, i):
    if i < NT2:
        return 2 * T1 + role * T2 + i * Q
    return 2 * T1 + 2 * T2 + (1 - role) * TC + (i - NT2) * Q


def kernel(
    u_hbm, l_hbm, picks_ref, out_ref,
    u, lab, hsq, recv, relay, onecol, pc, pr, ps, py, pz, pp, pq, pmat, psq,
    usq, res, inres, comb, incomb,
    loc_sem, lsem, m1s, m1r, m2s, m2r, p1s, p1r, p2s, p2r, p3s, p3r, ys, yr,
    xs, xr, gs, gr, rs, rr, fs, fr,
):
    g = lax.axis_index("grp")
    b = lax.axis_index("blk")
    yl = g // 2
    k = g % 2
    x = b % 4
    line = b // 4
    yh = line % 2
    z = line // 2

    def dev(yl_, b_, k_=None):
        return (yl_ * 2 + (k if k_ is None else k_), b_)

    def flip(c):
        return jnp.where(c, 1 - yl, yl)

    first, last = x == 0, x == 3
    core = dev(yl, b, 1 - k)
    yside = dev(1 - yl, b)
    ydiag = dev(1 - yl, b, 1 - k)
    back = dev(flip(first), (b + 31) % 32)
    ahead = dev(flip(last), (b + 1) % 32)
    back2 = dev(flip(x < 2), (b + 30) % 32)
    ahead2 = dev(flip(x >= 2), (b + 2) % 32)
    xp = [dev(yl, line * 4 + (x + d) % 4) for d in (1, 2, 3)]
    srcx = (x + 3) % 4
    onward = dev(flip(srcx < 2), (line * 4 + srcx + 30) % 32)
    far = (b + 2) % 32
    server = dev(flip(x >= 2), far // 4 * 4 + (far % 4 + 1) % 4)
    hi = dev(1 - yl, (z * 2 + (1 - yh)) * 4 + x)
    zp = [dev(yl, (((z + d) % 4) * 2 + yh) * 4 + x) for d in (1, 2, 3)]
    role1 = jnp.where(last, 1 - yl, yl)
    role2 = jnp.where(x >= 2, 1 - yl, yl)
    roles = (role1, role2)

    def local(src, dst, i):
        return pltpu.make_async_copy(src, dst, loc_sem.at[i])

    def remote(src, dst, s, r, to):
        return pltpu.make_async_remote_copy(
            src_ref=src, dst_ref=dst, send_sem=s, recv_sem=r,
            device_id=to, device_id_type=MESH,
        )

    def rows(ref, off):
        return ref.at[pl.ds(pl.multiple_of(off, Q), Q)]

    load_u = local(u_hbm, u, 0)
    load_l = local(l_hbm, lab.at[0], 1)
    load_u.start()
    load_l.start()

    peers = [core, yside, ydiag, back, ahead, back2, ahead2, onward, server, hi] + xp + zp
    barrier = pltpu.get_barrier_semaphore()
    for to in peers:
        pl.semaphore_signal(barrier, inc=1, device_id=to, device_id_type=MESH)
    pl.semaphore_wait(barrier, len(peers))

    started = []

    def go(copy):
        copy.start()
        started.append(copy)

    def minus1(i):
        off = minus_off(yl, i)
        return remote(rows(u_hbm, k * HALF + off), rows(recv.at[0], off), m1s.at[i], m1r.at[i], back)

    def minus1_in(i):
        ref = rows(recv.at[0], minus_off(role1, i))
        return remote(ref, ref, m1s.at[i], m1r.at[i], back)

    def minus2(i):
        off = minus_off(role1, i)
        return remote(rows(recv.at[0], off), rows(recv.at[1], off), m2s.at[i], m2r.at[i], back)

    def minus2_in(i):
        ref = rows(recv.at[1], minus_off(role2, i))
        return remote(ref, ref, m2s.at[i], m2r.at[i], back)

    def plus1(i):
        off = plus_off(yl, i)
        return remote(rows(u_hbm, k * HALF + off), relay.at[pl.ds(i * Q, Q)], p1s.at[i], p1r.at[i], xp[0])

    def plus2(i):
        off = plus_off(yl, i)
        return remote(relay.at[pl.ds(i * Q, Q)], rows(recv.at[1], off), p2s.at[i], p2r.at[i], onward)

    def plus2_in(i):
        ref = rows(recv.at[1], plus_off(role2, i))
        return remote(ref, ref, p2s.at[i], p2r.at[i], onward)

    def plus3(i):
        off = plus_off(role2, i)
        return remote(rows(recv.at[1], off), rows(recv.at[0], off), p3s.at[i], p3r.at[i], ahead)

    def plus3_in(i):
        ref = rows(recv.at[0], plus_off(role1, i))
        return remote(ref, ref, p3s.at[i], p3r.at[i], ahead)

    def across(s, j):
        role = roles[s]
        off = minus_off(role, j) if j < NT1 else plus_off(role, j - NT1)
        ref = rows(recv.at[s], off)
        return remote(ref, ref, ys.at[s, j], yr.at[s, j], yside)

    def across_in(s, j):
        role = 1 - roles[s]
        off = minus_off(role, j) if j < NT1 else plus_off(role, j - NT1)
        ref = rows(recv.at[s], off)
        return remote(ref, ref, ys.at[s, j], yr.at[s, j], yside)

    def on_m1(i):
        minus1_in(i).wait_recv()
        if i < NT1:
            go(across(0, i))
        go(minus2(i))

    def on_m2(i):
        minus2_in(i).wait_recv()
        if i < NT1:
            go(across(1, i))

    def on_p1(i):
        plus1(i).wait_recv()
        go(plus2(i))

    def on_p2(i):
        plus2_in(i).wait_recv()
        go(plus3(i))
        if i < NT2:
            go(across(1, NT1 + i))

    def on_p3(i):
        plus3_in(i).wait_recv()
        if i < NT2:
            go(across(0, NT1 + i))

    def on_y(s, js):
        for j in js:
            across_in(s, j).wait_recv()

    t1s = range(NT1)
    t2s = range(NT1, NT1 + NT2)

    swap_l = remote(l_hbm, lab.at[1], lsem.at[0], lsem.at[1], core)
    go(swap_l)
    for i in range(max(NM, NP)):
        if i < NM:
            go(minus1(i))
        if i < NP:
            go(plus1(i))

    quarter = (yl + yh) % 2 * 2 + k
    wide = jnp.broadcast_to(picks_ref[...], (128, 128))
    onecol[...] = wide.T
    mine = onecol[pl.ds(pl.multiple_of(quarter * PK, PK), PK), :]
    lane = lax.broadcasted_iota(jnp.int32, (PK, 128), 1)
    n_rows = u.shape[0]
    load_u.wait()
    KT = 512

    for j in range(4):
        def gather(t, acc):
            base = b * n_rows + t * KT
            hot = jnp.concatenate(
                [jnp.where(mine == lane + (base + c * 128), 1.0, 0.0) for c in range(KT // 128)], axis=1
            ).astype(BF16)
            return acc + jnp.dot(
                hot, u[pl.ds(pl.multiple_of(t * KT, KT), KT), j * 256:(j + 1) * 256],
                preferred_element_type=F32,
            )
        pc[j] = lax.fori_loop(0, n_rows // KT, gather, jnp.zeros((PK, 256), F32)).astype(BF16)

    def pick_x(d):
        return remote(pc.at[(x + d) % 4], pr.at[d - 1], xs.at[d - 1], xr.at[d - 1], xp[d - 1])

    def pick_y():
        return remote(ps.at[0], py, xs.at[3], xr.at[3], hi)

    def pick_z(d):
        return remote(ps.at[1], pz.at[d - 1], xs.at[3 + d], xr.at[3 + d], zp[d - 1])

    def pick_g(d):
        return remote(pp.at[x], pp.at[x], gs.at[d - 1], gr.at[d - 1], xp[d - 1])

    def pick_g_in(d):
        ref = pp.at[(x + 4 - d) % 4]
        return remote(ref, ref, gs.at[d - 1], gr.at[d - 1], xp[d - 1])

    def pick_c():
        return remote(pp, pq, gs.at[3], gr.at[3], core)

    for d in (1, 2, 3):
        go(pick_x(d))

    def half_squares(i):
        def step(t, c):
            r = pl.ds(pl.multiple_of(t * 128, 128), 128)
            w = lab[i, r, :].astype(F32)
            s = 0.5 * jnp.sum(w * w, axis=1, keepdims=True)
            hsq[pl.ds(pl.multiple_of(i * HALF + t * 128, 128), 128), :] = jnp.broadcast_to(s, (128, 128))
            return c
        lax.fori_loop(0, HALF // 128, step, 0)

    def task(src, slot, n=COLS):
        def step(t, best):
            h = hsq[pl.ds(pl.multiple_of(t * LT, LT), LT), :]
            i, r = t // (HALF // LT), t % (HALF // LT)
            v = lab[i, pl.ds(pl.multiple_of(r * LT, LT), LT), :]
            inner = lax.dot_general(v, src[...], (((1,), (1,)), ((), ())), preferred_element_type=F32)
            parts = []
            for c in range(n // 128):
                part = h - inner[:, c * 128:(c + 1) * 128]
                parts.append(jnp.min(part.reshape(LT // 8, 8, 128), axis=0))
            return jnp.minimum(best, jnp.concatenate(parts, axis=1))
        best = lax.fori_loop(0, 2 * HALF // LT, step, jnp.full((8, n), jnp.inf, F32))
        best = jnp.min(best, axis=0, keepdims=True)
        s, row = slot
        for c in range(n // 128):
            res[s, pl.ds(row + c, 1), :] = best[:, c * 128:(c + 1) * 128]

    def own(j):
        task(u.at[pl.ds(pl.multiple_of(k * HALF + j * COLS, COLS), COLS)], (2, 2 * j))

    def got_t1(s, role):
        task(recv.at[s, pl.ds(pl.multiple_of(role * T1, T1), T1)], (s, 2 * role))

    def got_t2(s):
        task(recv.at[s, pl.ds(2 * T1, COLS)], (s, 4))

    def got_c(s):
        task(recv.at[s, pl.ds(2 * T1 + 2 * T2, COLS)], (s, 6))

    def result(s):
        to = (ahead, ahead2)[s]
        return remote(res.at[s], inres.at[s], rs.at[s], rr.at[s], to)

    load_l.wait()
    half_squares(0)
    on_m1(0)
    on_p1(0)

    def own_squares(i, c):
        w = u[pl.ds(pl.multiple_of(k * HALF + i * 128, 128), 128), :].astype(F32)
        w = w * w
        s = w[:, 0:128]
        for c_ in range(1, D // 128):
            s = s + w[:, c_ * 128:(c_ + 1) * 128]
        usq[pl.ds(i, 1), :] = jnp.sum(s.T, axis=0, keepdims=True)
        return c
    lax.fori_loop(0, HALF // 128, own_squares, 0)
    swap_l.wait_recv()
    half_squares(1)
    on_m1(1)
    on_p1(1)
    for d in (1, 2, 3):
        pick_x(d).wait_recv()
    ps[0] = pc[x] + pr[0] + pr[1] + pr[2]
    go(pick_y())
    own(0)
    own(1)
    on_m1(2)
    on_p1(2)
    pick_y().wait_recv()
    ps[1] = ps[0] + py[...]
    for d in (1, 2, 3):
        go(pick_z(d))
    own(2)
    on_m1(3)
    on_p1(3)
    for d in (1, 2, 3):
        pick_z(d).wait_recv()
    pp[x] = ps[1] + pz[0] + pz[1] + pz[2]
    for d in (1, 2, 3):
        go(pick_g(d))
    own(3)
    on_m1(4)
    on_p2(0)
    got_t1(0, role1)
    on_m1(5)
    on_p2(1)
    for d in (1, 2, 3):
        pick_g_in(d).wait_recv()
    go(pick_c())
    on_y(0, t1s)
    got_t1(0, 1 - role1)
    on_m2(0)
    on_p2(2)
    on_y(1, t2s)
    got_t2(1)
    on_m2(1)
    on_p2(3)

    pick_c().wait_recv()
    for j in range(4):
        pmat[0:PK, j * 256:(j + 1) * 256] = pp[j]
        pmat[PK:2 * PK, j * 256:(j + 1) * 256] = pq[j]
    w = pmat[...].astype(F32)
    psq[...] = jnp.broadcast_to(0.5 * jnp.sum(w * w, axis=1, keepdims=True), (2 * PK, 128))

    def pick_task(j, c):
        v = u[pl.ds(pl.multiple_of(k * HALF + j * COLS, COLS), COLS), :]
        inner = lax.dot_general(pmat[...], v, (((1,), (1,)), ((), ())), preferred_element_type=F32)
        for c_ in range(COLS // 128):
            part = jnp.min(psq[...] - inner[:, c_ * 128:(c_ + 1) * 128], axis=0, keepdims=True)
            at = pl.ds(2 * j + c_, 1)
            res[2, at, :] = jnp.minimum(res[2, at, :], part)
        return c
    lax.fori_loop(0, HALF // COLS, pick_task, 0)

    on_m2(2)
    on_p3(0)
    on_m2(3)
    on_p3(1)
    got_t1(1, role2)
    on_m2(4)
    on_p3(2)
    on_y(1, t1s)
    got_t1(1, 1 - role2)
    on_m2(5)
    on_p3(3)
    got_c(1)
    go(result(1))
    got_c(0)
    on_y(0, t2s)
    got_t2(0)
    go(result(0))

    result(1).wait_recv()
    result(0).wait_recv()
    least = jnp.minimum(jnp.minimum(inres[0], inres[1]), res[2])
    comb[...] = (usq[...] + 2.0 * least) * (1.0 / D)
    finals = [
        remote(comb, incomb.at[i], fs.at[i], fr.at[i], to)
        for i, to in enumerate((core, yside, ydiag))
    ]
    for copy in finals:
        go(copy)
    for copy in finals:
        copy.wait_recv()
    out_ref[k] = jnp.minimum(comb[...], incomb[1])
    out_ref[1 - k] = jnp.minimum(incomb[0], incomb[2])
    for copy in started:
        copy.wait_send()


def body(unlabeled, labeled, picks):
    n_rows = unlabeled.shape[0]
    dma = pltpu.SemaphoreType.DMA
    vm = pltpu.VMEM
    out = pl.pallas_call(
        kernel,
        out_shape=jax.ShapeDtypeStruct((2, 8, 128), F32),
        in_specs=[
            pl.BlockSpec(memory_space=pl.ANY),
            pl.BlockSpec(memory_space=pl.ANY),
            pl.BlockSpec(memory_space=pltpu.VMEM),
        ],
        out_specs=pl.BlockSpec(memory_space=pltpu.VMEM),
        scratch_shapes=[
            vm((n_rows, D), BF16), vm((2, HALF, D), BF16), vm((2 * HALF, 128), F32),
            vm((2, HALF, D), BF16), vm((NP * Q, D), BF16), vm((128, 128), jnp.int32),
            vm((4, PK, 256), BF16), vm((3, PK, 256), BF16), vm((2, PK, 256), BF16),
            vm((PK, 256), BF16), vm((3, PK, 256), BF16), vm((4, PK, 256), BF16),
            vm((4, PK, 256), BF16), vm((2 * PK, D), BF16), vm((2 * PK, 128), F32),
            vm((8, 128), F32), vm((3, 8, 128), F32), vm((2, 8, 128), F32),
            vm((8, 128), F32), vm((3, 8, 128), F32),
            dma((2,)), dma((2,)), dma((NM,)), dma((NM,)), dma((NM,)), dma((NM,)),
            dma((NP,)), dma((NP,)), dma((NP,)), dma((NP,)), dma((NP,)), dma((NP,)),
            dma((2, NT1 + NT2)), dma((2, NT1 + NT2)),
            dma((7,)), dma((7,)), dma((4,)), dma((4,)), dma((2,)), dma((2,)), dma((3,)), dma((3,)),
        ],
        compiler_params=pltpu.CompilerParams(
            collective_id=0, has_side_effects=True, vmem_limit_bytes=48 << 20
        ),
    )(unlabeled, labeled, picks.reshape(1, -1))
    return out.reshape(-1)


def solution(mesh):
    return jax.shard_map(
        body,
        mesh=mesh,
        in_specs=(P("blk", None), P(("grp", "blk"), None), P()),
        out_specs=P("blk"),
        check_vma=False,
    )
```

```python
import jax
import jax.numpy as jnp
from jax import lax
from jax.experimental import pallas as pl
from jax.experimental.pallas import tpu as pltpu
from jax.sharding import PartitionSpec as P

MESH = pl.DeviceIdType.MESH
F32 = jnp.float32
BF16 = jnp.bfloat16

D = 1024
HALF = 1024
T1 = 256
T2 = 128
TC = 128
Q = 32
AHEAD = 3
NM = (T1 + TC) // Q
NP = (T2 + TC) // Q
NT1 = T1 // Q
NT2 = T2 // Q
PK = 32
LT = 512
COLS = 256

ORDER = (
    ("gather",), ("hsq0",), ("usq",), ("m1", 0), ("p1", 0), ("m1", 1), ("p1", 1), ("L", 0), ("hsq1",),
    ("y0", 0), ("m1", 2), ("p1", 2), ("own0",), ("y0", 1), ("m1", 3), ("p1", 3), ("own1",), ("y0", 2),
    ("m2", 0), ("p2", 0), ("own2",), ("m1", 4), ("p1", 4), ("y0", 3), ("m2", 1), ("p2", 1), ("own3",),
    ("y1", 0), ("m1", 5), ("p1", 5), ("y1", 8), ("m2", 2), ("p2", 2), ("y0", 4), ("m1", 6), ("p1", 6),
    ("y1", 1), ("m2", 3), ("p2", 3), ("px", 0), ("y1", 9), ("p3", 0), ("m1", 7), ("A0",), ("y0", 5),
    ("m2", 4), ("p1", 7), ("y1", 2), ("p2", 4), ("m1", 8), ("y1", 10), ("p3", 1), ("m2", 5), ("y0", 6),
    ("p2", 5), ("m1", 9), ("py", 0), ("y1", 3), ("p3", 2), ("m2", 6), ("y1", 11), ("E1",), ("p2", 6),
    ("m1", 10), ("y0", 8), ("p3", 3), ("m2", 7), ("A1",), ("y0", 7), ("p2", 7), ("m1", 11), ("y1", 4),
    ("B0",), ("p3", 4), ("m2", 8), ("y0", 9), ("p3", 5), ("m2", 9), ("pz", 0), ("y1", 5), ("p3", 6),
    ("m2", 10), ("y0", 10), ("p3", 7), ("m2", 11), ("F1",), ("y1", 6), ("F0",), ("y0", 11), ("y1", 7),
    ("B1",), ("E0",), ("pg", 0), ("pc", 0), ("psq",), ("ptask",),
)


def minus_off(role, i):
    if i < NT1:
        return role * T1 + i * Q
    return 2 * T1 + 2 * T2 + role * TC + (i - NT1) * Q


def plus_off(role, i):
    if i < NT2:
        return 2 * T1 + role * T2 + i * Q
    return 2 * T1 + 2 * T2 + (1 - role) * TC + (i - NT2) * Q


def kernel(
    u_hbm, l_hbm, picks_ref, out_ref,
    u, lab, hsq, recv, relay, onecol, pc, pr, ps, py, pz, pp, pq, pmat, psq,
    usq, res, inres, comb, incomb,
    loc_sem, lsem, m1s, m1r, m2s, m2r, p1s, p1r, p2s, p2r, p3s, p3r, ys, yr,
    xs, xr, gs, gr, rs, rr, fs, fr,
):
    g = lax.axis_index("grp")
    b = lax.axis_index("blk")
    yl = g // 2
    k = g % 2
    x = b % 4
    line = b // 4
    yh = line % 2
    z = line // 2

    def dev(yl_, b_, k_=None):
        return (yl_ * 2 + (k if k_ is None else k_), b_)

    def flip(c):
        return jnp.where(c, 1 - yl, yl)

    first, last = x == 0, x == 3
    core = dev(yl, b, 1 - k)
    yside = dev(1 - yl, b)
    ydiag = dev(1 - yl, b, 1 - k)
    back = dev(flip(first), (b + 31) % 32)
    ahead = dev(flip(last), (b + 1) % 32)
    back2 = dev(flip(x < 2), (b + 30) % 32)
    ahead2 = dev(flip(x >= 2), (b + 2) % 32)
    xp = [dev(yl, line * 4 + (x + d) % 4) for d in (1, 2, 3)]
    relay_to = dev(flip(x < 2), jnp.where(x < 2, (b + 29) % 32, line * 4 + (x + 1) % 4))
    fed = (x == 1) | (x == 2)
    relay_from = dev(flip(fed), jnp.where(fed, (b + 3) % 32, line * 4 + (x + 3) % 4))
    relay_role = flip(fed)
    hi = dev(1 - yl, (z * 2 + (1 - yh)) * 4 + x)
    zp = [dev(yl, (((z + d) % 4) * 2 + yh) * 4 + x) for d in (1, 2, 3)]
    role1 = jnp.where(last, 1 - yl, yl)
    role2 = jnp.where(x >= 2, 1 - yl, yl)
    roles = (role1, role2)

    def local(src, dst, i):
        return pltpu.make_async_copy(src, dst, loc_sem.at[i])

    def remote(src, dst, s, r, to):
        return pltpu.make_async_remote_copy(
            src_ref=src, dst_ref=dst, send_sem=s, recv_sem=r,
            device_id=to, device_id_type=MESH,
        )

    def rows(ref, off):
        return ref.at[pl.ds(pl.multiple_of(off, Q), Q)]

    load_u = local(u_hbm, u, 0)
    load_l = local(l_hbm, lab.at[0], 1)
    load_u.start()
    load_l.start()

    peers = [core, yside, ydiag, back, ahead, back2, ahead2, relay_to, relay_from, hi] + xp + zp
    barrier = pltpu.get_barrier_semaphore()
    for to in peers:
        pl.semaphore_signal(barrier, inc=1, device_id=to, device_id_type=MESH)
    pl.semaphore_wait(barrier, len(peers))

    started = []

    def go(copy):
        copy.start()
        started.append(copy)

    def minus1(i):
        off = minus_off(yl, i)
        return remote(rows(u_hbm, k * HALF + off), rows(recv.at[0], off), m1s.at[i], m1r.at[i], back)

    def minus1_in(i):
        ref = rows(recv.at[0], minus_off(role1, i))
        return remote(ref, ref, m1s.at[i], m1r.at[i], back)

    def minus2(i):
        off = minus_off(role1, i)
        return remote(rows(recv.at[0], off), rows(recv.at[1], off), m2s.at[i], m2r.at[i], back)

    def minus2_in(i):
        ref = rows(recv.at[1], minus_off(role2, i))
        return remote(ref, ref, m2s.at[i], m2r.at[i], back)

    def plus1(i):
        off = plus_off(yl, i)
        return remote(rows(u_hbm, k * HALF + off), relay.at[pl.ds(i * Q, Q)], p1s.at[i], p1r.at[i], relay_to)

    def plus2(i):
        off = plus_off(relay_role, i)
        return remote(relay.at[pl.ds(i * Q, Q)], rows(recv.at[1], off), p2s.at[i], p2r.at[i], xp[0])

    def plus2_in(i):
        ref = rows(recv.at[1], plus_off(role2, i))
        return remote(ref, ref, p2s.at[i], p2r.at[i], xp[0])

    def plus3(i):
        off = plus_off(role2, i)
        return remote(rows(recv.at[1], off), rows(recv.at[0], off), p3s.at[i], p3r.at[i], ahead)

    def plus3_in(i):
        ref = rows(recv.at[0], plus_off(role1, i))
        return remote(ref, ref, p3s.at[i], p3r.at[i], ahead)

    def across(s, j):
        role = roles[s]
        off = minus_off(role, j) if j < NT1 else plus_off(role, j - NT1)
        ref = rows(recv.at[s], off)
        return remote(ref, ref, ys.at[s, j], yr.at[s, j], yside)

    def across_in(s, j):
        role = 1 - roles[s]
        off = minus_off(role, j) if j < NT1 else plus_off(role, j - NT1)
        ref = rows(recv.at[s], off)
        return remote(ref, ref, ys.at[s, j], yr.at[s, j], yside)

    def on_m1(i):
        minus1_in(i).wait_recv()
        if i < NT1:
            go(across(0, i))
        if i + AHEAD < NM:
            go(minus1(i + AHEAD))
        go(minus2(i))

    def on_m2(i):
        minus2_in(i).wait_recv()
        if i < NT1:
            go(across(1, i))

    def on_p1(i):
        plus1(i).wait_recv()
        if i + AHEAD < NP:
            go(plus1(i + AHEAD))
        go(plus2(i))

    def on_p2(i):
        plus2_in(i).wait_recv()
        go(plus3(i))
        if i < NT2:
            go(across(1, NT1 + i))

    def on_p3(i):
        plus3_in(i).wait_recv()
        if i < NT2:
            go(across(0, NT1 + i))

    swap_l = remote(l_hbm, lab.at[1], lsem.at[0], lsem.at[1], core)
    go(swap_l)
    for i in range(min(AHEAD, NM)):
        if i < NM:
            go(minus1(i))
        if i < NP:
            go(plus1(i))

    quarter = (yl + yh) % 2 * 2 + k
    wide = jnp.broadcast_to(picks_ref[...], (128, 128))
    onecol[...] = wide.T
    mine = onecol[pl.ds(pl.multiple_of(quarter * PK, PK), PK), :]
    lane = lax.broadcasted_iota(jnp.int32, (PK, 128), 1)
    n_rows = u.shape[0]
    KT = 512

    def gather_picks():
        load_u.wait()
        acc = jnp.zeros((PK, D), F32)
        for t in range(n_rows // KT):
            base = b * n_rows + t * KT
            hot = jnp.concatenate(
                [jnp.where(mine == lane + (base + c * 128), 1.0, 0.0) for c in range(KT // 128)], axis=1
            ).astype(BF16)
            acc = acc + jnp.dot(hot, u[t * KT:(t + 1) * KT, :], preferred_element_type=F32)
        for j in range(4):
            pc[j] = acc[:, j * 256:(j + 1) * 256].astype(BF16)
        for d in (1, 2, 3):
            go(pick_x(d))

    def pick_x(d):
        return remote(pc.at[(x + d) % 4], pr.at[d - 1], xs.at[d - 1], xr.at[d - 1], xp[d - 1])

    def pick_y():
        return remote(ps.at[0], py, xs.at[3], xr.at[3], hi)

    def pick_z(d):
        return remote(ps.at[1], pz.at[d - 1], xs.at[3 + d], xr.at[3 + d], zp[d - 1])

    def pick_g(d):
        return remote(pp.at[x], pp.at[x], gs.at[d - 1], gr.at[d - 1], xp[d - 1])

    def pick_g_in(d):
        ref = pp.at[(x + 4 - d) % 4]
        return remote(ref, ref, gs.at[d - 1], gr.at[d - 1], xp[d - 1])

    def pick_c():
        return remote(pp, pq, gs.at[3], gr.at[3], core)

    def half_squares(i):
        def step(t, c):
            r = pl.ds(pl.multiple_of(t * 128, 128), 128)
            w = lab[i, r, :].astype(F32)
            s = 0.5 * jnp.sum(w * w, axis=1, keepdims=True)
            hsq[pl.ds(pl.multiple_of(i * HALF + t * 128, 128), 128), :] = jnp.broadcast_to(s, (128, 128))
            return c
        lax.fori_loop(0, HALF // 128, step, 0)

    def task(src, slot, n=COLS):
        best = jnp.full((8, n), jnp.inf, F32)
        for t in range(2 * HALF // LT):
            h = hsq[t * LT:(t + 1) * LT, :]
            i, r = t // (HALF // LT), t % (HALF // LT)
            v = lab[i, r * LT:(r + 1) * LT, :]
            inner = lax.dot_general(v, src[...], (((1,), (1,)), ((), ())), preferred_element_type=F32)
            parts = []
            for c in range(n // 128):
                part = h - inner[:, c * 128:(c + 1) * 128]
                parts.append(jnp.min(part.reshape(LT // 8, 8, 128), axis=0))
            best = jnp.minimum(best, jnp.concatenate(parts, axis=1))
        best = jnp.min(best, axis=0, keepdims=True)
        s, row = slot
        for c in range(n // 128):
            res[s, pl.ds(row + c, 1), :] = best[:, c * 128:(c + 1) * 128]

    def own(j):
        task(u.at[pl.ds(pl.multiple_of(k * HALF + j * COLS, COLS), COLS)], (2, 2 * j))

    def got_t1(s, role):
        task(recv.at[s, pl.ds(pl.multiple_of(role * T1, T1), T1)], (s, 2 * role))

    def got_t2(s):
        task(recv.at[s, pl.ds(2 * T1, COLS)], (s, 4))

    def got_c(s):
        task(recv.at[s, pl.ds(2 * T1 + 2 * T2, COLS)], (s, 6))

    def result(s):
        to = (ahead, ahead2)[s]
        return remote(res.at[s], inres.at[s], rs.at[s], rr.at[s], to)

    def own_squares():
        def step(i, c):
            w = u[pl.ds(pl.multiple_of(k * HALF + i * 128, 128), 128), :].astype(F32)
            w = w * w
            t = w[:, 0:128]
            for c_ in range(1, D // 128):
                t = t + w[:, c_ * 128:(c_ + 1) * 128]
            usq[pl.ds(i, 1), :] = jnp.sum(t.T, axis=0, keepdims=True)
            return c
        lax.fori_loop(0, HALF // 128, step, 0)

    def first_half_squares():
        load_l.wait()
        half_squares(0)

    def on_px(i):
        for d in (1, 2, 3):
            pick_x(d).wait_recv()
        ps[0] = pc[x] + pr[0] + pr[1] + pr[2]
        go(pick_y())

    def on_py(i):
        pick_y().wait_recv()
        ps[1] = ps[0] + py[...]
        for d in (1, 2, 3):
            go(pick_z(d))

    def on_pz(i):
        for d in (1, 2, 3):
            pick_z(d).wait_recv()
        pp[x] = ps[1] + pz[0] + pz[1] + pz[2]
        for d in (1, 2, 3):
            go(pick_g(d))

    def on_pg(i):
        for d in (1, 2, 3):
            pick_g_in(d).wait_recv()
        go(pick_c())

    def pick_squares():
        for j in range(4):
            pmat[0:PK, j * 256:(j + 1) * 256] = pp[j]
            pmat[PK:2 * PK, j * 256:(j + 1) * 256] = pq[j]
        w = pmat[...].astype(F32)
        psq[...] = jnp.broadcast_to(0.5 * jnp.sum(w * w, axis=1, keepdims=True), (2 * PK, 128))

    def pick_tasks():
        for j in range(HALF // COLS):
            v = u[pl.ds(pl.multiple_of(k * HALF + j * COLS, COLS), COLS), :]
            inner = lax.dot_general(pmat[...], v, (((1,), (1,)), ((), ())), preferred_element_type=F32)
            for c in range(COLS // 128):
                part = jnp.min(psq[...] - inner[:, c * 128:(c + 1) * 128], axis=0, keepdims=True)
                row = 2 * j + c
                res[2, row:row + 1, :] = jnp.minimum(res[2, row:row + 1, :], part)

    events = {
        "m1": on_m1, "m2": on_m2, "p1": on_p1, "p2": on_p2, "p3": on_p3,
        "y0": lambda i: across_in(0, i).wait_recv(), "y1": lambda i: across_in(1, i).wait_recv(),
        "L": lambda i: swap_l.wait_recv(),
        "px": on_px, "py": on_py, "pz": on_pz, "pg": on_pg, "pc": lambda i: pick_c().wait_recv(),
    }
    work = {
        "gather": gather_picks, "hsq0": first_half_squares, "hsq1": lambda: half_squares(1),
        "usq": own_squares, "psq": pick_squares, "ptask": pick_tasks,
        "own0": lambda: own(0), "own1": lambda: own(1), "own2": lambda: own(2), "own3": lambda: own(3),
        "A0": lambda: got_t1(0, role1), "A1": lambda: got_t1(1, role2),
        "B0": lambda: got_t1(0, 1 - role1), "B1": lambda: got_t1(1, 1 - role2),
        "E0": lambda: got_t2(0), "E1": lambda: got_t2(1), "F0": lambda: got_c(0), "F1": lambda: got_c(1),
    }
    finished = [0, 0]
    for step in ORDER:
        if len(step) == 2:
            events[step[0]](step[1])
        else:
            work[step[0]]()
            if step[0][0] in "ABEF":
                s = int(step[0][1])
                finished[s] += 1
                if finished[s] == 4:
                    go(result(s))

    result(1).wait_recv()
    result(0).wait_recv()
    least = jnp.minimum(jnp.minimum(inres[0], inres[1]), res[2])
    comb[...] = (usq[...] + 2.0 * least) * (1.0 / D)
    finals = [
        remote(comb, incomb.at[i], fs.at[i], fr.at[i], to)
        for i, to in enumerate((core, yside, ydiag))
    ]
    for copy in finals:
        go(copy)
    for copy in finals:
        copy.wait_recv()
    out_ref[k] = jnp.minimum(comb[...], incomb[1])
    out_ref[1 - k] = jnp.minimum(incomb[0], incomb[2])
    for copy in started:
        copy.wait_send()


def body(unlabeled, labeled, picks):
    n_rows = unlabeled.shape[0]
    dma = pltpu.SemaphoreType.DMA
    vm = pltpu.VMEM
    out = pl.pallas_call(
        kernel,
        out_shape=jax.ShapeDtypeStruct((2, 8, 128), F32),
        in_specs=[
            pl.BlockSpec(memory_space=pl.ANY),
            pl.BlockSpec(memory_space=pl.ANY),
            pl.BlockSpec(memory_space=pltpu.VMEM),
        ],
        out_specs=pl.BlockSpec(memory_space=pltpu.VMEM),
        scratch_shapes=[
            vm((n_rows, D), BF16), vm((2, HALF, D), BF16), vm((2 * HALF, 128), F32),
            vm((2, HALF, D), BF16), vm((NP * Q, D), BF16), vm((128, 128), jnp.int32),
            vm((4, PK, 256), BF16), vm((3, PK, 256), BF16), vm((2, PK, 256), BF16),
            vm((PK, 256), BF16), vm((3, PK, 256), BF16), vm((4, PK, 256), BF16),
            vm((4, PK, 256), BF16), vm((2 * PK, D), BF16), vm((2 * PK, 128), F32),
            vm((8, 128), F32), vm((3, 8, 128), F32), vm((2, 8, 128), F32),
            vm((8, 128), F32), vm((3, 8, 128), F32),
            dma((2,)), dma((2,)), dma((NM,)), dma((NM,)), dma((NM,)), dma((NM,)),
            dma((NP,)), dma((NP,)), dma((NP,)), dma((NP,)), dma((NP,)), dma((NP,)),
            dma((2, NT1 + NT2)), dma((2, NT1 + NT2)),
            dma((7,)), dma((7,)), dma((4,)), dma((4,)), dma((2,)), dma((2,)), dma((3,)), dma((3,)),
        ],
        compiler_params=pltpu.CompilerParams(
            collective_id=0, has_side_effects=True, vmem_limit_bytes=60 << 20
        ),
    )(unlabeled, labeled, picks.reshape(1, -1))
    return out.reshape(-1)


def solution(mesh):
    return jax.shard_map(
        body,
        mesh=mesh,
        in_specs=(P("blk", None), P(("grp", "blk"), None), P()),
        out_specs=P("blk"),
        check_vma=False,
    )
```

```python
import jax
import jax.numpy as jnp
from jax import lax
from jax.experimental import pallas as pl
from jax.experimental.pallas import tpu as pltpu
from jax.sharding import PartitionSpec as P

MESH = pl.DeviceIdType.MESH
F32 = jnp.float32
BF16 = jnp.bfloat16

D = 1024
HALF = 1024
T1 = 256
T2 = 128
TC = 128
Q = 32
AHEAD = 3
LAST = 5
NM = (T1 + TC) // Q
NP = (T2 + TC) // Q
NT1 = T1 // Q
NT2 = T2 // Q
PK = 32
LT = 512
COLS = 256

ORDER = (
    ("gather",), ("hsq0",), ("usq",), ("m1", 0), ("p1", 0), ("m1", 1), ("p1", 1), ("L", 0), ("hsq1",),
    ("y0", 0), ("m1", 2), ("p1", 2), ("own0",), ("y0", 1), ("m1", 3), ("p1", 3), ("own1",), ("y0", 2),
    ("m2", 0), ("p2", 0), ("own2",), ("m1", 4), ("p1", 4), ("y0", 3), ("m2", 1), ("p2", 1), ("own3",),
    ("y1", 0), ("m1", 5), ("p1", 5), ("y1", 8), ("m2", 2), ("p2", 2), ("y0", 4), ("m1", 6), ("p1", 6),
    ("y1", 1), ("m2", 3), ("p2", 3), ("y1", 9), ("p3", 0), ("m1", 7), ("A0",), ("y0", 5), ("m2", 4),
    ("p1", 7), ("y1", 2), ("p2", 4), ("m1", 8), ("y1", 10), ("p3", 1), ("m2", 5), ("px", 0), ("y0", 6),
    ("p2", 5), ("m1", 9), ("y1", 11), ("E1",), ("p3", 2), ("m2", 6), ("y0", 8), ("p2", 6), ("m1", 10),
    ("y0", 7), ("B0",), ("p3", 3), ("m2", 7), ("y0", 9), ("p2", 7), ("m1", 11), ("py", 0), ("A1",),
    ("y0", 10), ("p3", 4), ("m2", 8), ("y0", 11), ("E0",), ("p3", 5), ("m2", 9), ("y1", 3), ("p3", 6),
    ("m2", 10), ("y1", 4), ("p3", 7), ("m2", 11), ("F1",), ("y1", 5), ("pz", 0), ("F0",), ("y1", 6),
    ("y1", 7), ("B1",), ("pg", 0), ("pc", 0), ("psq",), ("ptask",),
)


def minus_off(role, i):
    if i < NT1:
        return role * T1 + i * Q
    return 2 * T1 + 2 * T2 + role * TC + (i - NT1) * Q


def plus_off(role, i):
    if i < NT2:
        return 2 * T1 + role * T2 + i * Q
    return 2 * T1 + 2 * T2 + (1 - role) * TC + (i - NT2) * Q


def kernel(
    u_hbm, l_hbm, picks_ref, out_ref,
    u, lab, hsq, recv, relay, onecol, pc, pr, ps, py, pz, pp, pq, pmat, psq,
    res, got, kept, near,
    loc_sem, lsem, m1s, m1r, m2s, m2r, p1s, p1r, p2s, p2r, p3s, p3r, ys, yr,
    xs, xr, gs, gr, rs, rr, fs, fr,
):
    g = lax.axis_index("grp")
    b = lax.axis_index("blk")
    yl = g // 2
    k = g % 2
    x = b % 4
    line = b // 4
    yh = line % 2
    z = line // 2

    def dev(yl_, b_, k_=None):
        return (yl_ * 2 + (k if k_ is None else k_), b_)

    def flip(c):
        return jnp.where(c, 1 - yl, yl)

    first, last = x == 0, x == 3
    core = dev(yl, b, 1 - k)
    yside = dev(1 - yl, b)
    ydiag = dev(1 - yl, b, 1 - k)
    back = dev(flip(first), (b + 31) % 32)
    ahead = dev(flip(last), (b + 1) % 32)
    xp = [dev(yl, line * 4 + (x + d) % 4) for d in (1, 2, 3)]
    relay_to = dev(flip(x < 2), jnp.where(x < 2, (b + 29) % 32, line * 4 + (x + 1) % 4))
    fed = (x == 1) | (x == 2)
    relay_from = dev(flip(fed), jnp.where(fed, (b + 3) % 32, line * 4 + (x + 3) % 4))
    relay_role = flip(fed)
    hi = dev(1 - yl, (z * 2 + (1 - yh)) * 4 + x)
    zp = [dev(yl, (((z + d) % 4) * 2 + yh) * 4 + x) for d in (1, 2, 3)]
    role1 = jnp.where(last, 1 - yl, yl)
    role2 = jnp.where(x >= 2, 1 - yl, yl)
    roles = (role1, role2)

    def local(src, dst, i):
        return pltpu.make_async_copy(src, dst, loc_sem.at[i])

    def remote(src, dst, s, r, to):
        return pltpu.make_async_remote_copy(
            src_ref=src, dst_ref=dst, send_sem=s, recv_sem=r,
            device_id=to, device_id_type=MESH,
        )

    def rows(ref, off):
        return ref.at[pl.ds(pl.multiple_of(off, Q), Q)]

    load_u = local(u_hbm, u, 0)
    load_l = local(l_hbm, lab.at[0], 1)
    load_u.start()
    load_l.start()

    groups = [[(i, (b + d) % 32) for i in range(4)] for d in (1, 2, 30, 31)]
    peers = [core, yside, ydiag, relay_to, relay_from, hi] + xp + zp + sum(groups, [])
    barrier = pltpu.get_barrier_semaphore()
    for to in peers:
        pl.semaphore_signal(barrier, inc=1, device_id=to, device_id_type=MESH)
    pl.semaphore_wait(barrier, len(peers))

    started = []

    def go(copy):
        copy.start()
        started.append(copy)

    def minus1(i):
        off = minus_off(yl, i)
        return remote(rows(u_hbm, k * HALF + off), rows(recv.at[0], off), m1s.at[i], m1r.at[i], back)

    def minus1_in(i):
        ref = rows(recv.at[0], minus_off(role1, i))
        return remote(ref, ref, m1s.at[i], m1r.at[i], back)

    def minus2(i):
        off = minus_off(role1, i)
        return remote(rows(recv.at[0], off), rows(recv.at[1], off), m2s.at[i], m2r.at[i], back)

    def minus2_in(i):
        ref = rows(recv.at[1], minus_off(role2, i))
        return remote(ref, ref, m2s.at[i], m2r.at[i], back)

    def plus1(i):
        off = plus_off(yl, i)
        return remote(rows(u_hbm, k * HALF + off), relay.at[pl.ds(i * Q, Q)], p1s.at[i], p1r.at[i], relay_to)

    def plus2(i):
        off = plus_off(relay_role, i)
        return remote(relay.at[pl.ds(i * Q, Q)], rows(recv.at[1], off), p2s.at[i], p2r.at[i], xp[0])

    def plus2_in(i):
        ref = rows(recv.at[1], plus_off(role2, i))
        return remote(ref, ref, p2s.at[i], p2r.at[i], xp[0])

    def plus3(i):
        off = plus_off(role2, i)
        return remote(rows(recv.at[1], off), rows(recv.at[0], off), p3s.at[i], p3r.at[i], ahead)

    def plus3_in(i):
        ref = rows(recv.at[0], plus_off(role1, i))
        return remote(ref, ref, p3s.at[i], p3r.at[i], ahead)

    def across(s, j):
        role = roles[s]
        off = minus_off(role, j) if j < NT1 else plus_off(role, j - NT1)
        ref = rows(recv.at[s], off)
        return remote(ref, ref, ys.at[s, j], yr.at[s, j], yside)

    def across_in(s, j):
        role = 1 - roles[s]
        off = minus_off(role, j) if j < NT1 else plus_off(role, j - NT1)
        ref = rows(recv.at[s], off)
        return remote(ref, ref, ys.at[s, j], yr.at[s, j], yside)

    held, flushed = [], []

    def on_m1(i):
        minus1_in(i).wait_recv()
        if i < NT1:
            go(across(0, i))
        if i + AHEAD < NM:
            go(minus1(i + AHEAD))
        go(minus2(i))

    def on_m2(i):
        minus2_in(i).wait_recv()
        if i < NT1:
            if i >= NT1 - LAST and not flushed:
                held.append(i)
            else:
                go(across(1, i))

    def on_p1(i):
        plus1(i).wait_recv()
        if i + AHEAD < NP:
            go(plus1(i + AHEAD))
        go(plus2(i))

    def on_p2(i):
        plus2_in(i).wait_recv()
        go(plus3(i))
        if i < NT2:
            go(across(1, NT1 + i))

    def on_p3(i):
        plus3_in(i).wait_recv()
        if i < NT2:
            go(across(0, NT1 + i))
        if i == NT2 - 1:
            flushed.append(i)
            for j in held:
                go(across(1, j))

    swap_l = remote(l_hbm, lab.at[1], lsem.at[0], lsem.at[1], core)
    go(swap_l)
    for i in range(min(AHEAD, NM)):
        if i < NM:
            go(minus1(i))
        if i < NP:
            go(plus1(i))

    quarter = (yl + yh) % 2 * 2 + k
    wide = jnp.broadcast_to(picks_ref[...], (128, 128))
    onecol[...] = wide.T
    mine = onecol[pl.ds(pl.multiple_of(quarter * PK, PK), PK), :]
    lane = lax.broadcasted_iota(jnp.int32, (PK, 128), 1)
    n_rows = u.shape[0]
    KT = 512

    def gather_picks():
        load_u.wait()
        acc = jnp.zeros((PK, D), F32)
        for t in range(n_rows // KT):
            base = b * n_rows + t * KT
            hot = jnp.concatenate(
                [jnp.where(mine == lane + (base + c * 128), 1.0, 0.0) for c in range(KT // 128)], axis=1
            ).astype(BF16)
            acc = acc + jnp.dot(hot, u[t * KT:(t + 1) * KT, :], preferred_element_type=F32)
        for j in range(4):
            pc[j] = acc[:, j * 256:(j + 1) * 256].astype(BF16)
        for d in (1, 2, 3):
            go(pick_x(d))

    def pick_x(d):
        return remote(pc.at[(x + d) % 4], pr.at[d - 1], xs.at[d - 1], xr.at[d - 1], xp[d - 1])

    def pick_y():
        return remote(ps.at[0], py, xs.at[3], xr.at[3], hi)

    def pick_z(d):
        return remote(ps.at[1], pz.at[d - 1], xs.at[3 + d], xr.at[3 + d], zp[d - 1])

    def pick_g(d):
        return remote(pp.at[x], pp.at[x], gs.at[d - 1], gr.at[d - 1], xp[d - 1])

    def pick_g_in(d):
        ref = pp.at[(x + 4 - d) % 4]
        return remote(ref, ref, gs.at[d - 1], gr.at[d - 1], xp[d - 1])

    def pick_c():
        return remote(pp, pq, gs.at[3], gr.at[3], core)

    def half_squares(i):
        def step(t, c):
            r = pl.ds(pl.multiple_of(t * 128, 128), 128)
            w = lab[i, r, :].astype(F32)
            s = 0.5 * jnp.sum(w * w, axis=1, keepdims=True)
            hsq[pl.ds(pl.multiple_of(i * HALF + t * 128, 128), 128), :] = jnp.broadcast_to(s, (128, 128))
            return c
        lax.fori_loop(0, HALF // 128, step, 0)

    def task(src, slot, n=COLS):
        best = jnp.full((8, n), jnp.inf, F32)
        for t in range(2 * HALF // LT):
            h = hsq[t * LT:(t + 1) * LT, :]
            i, r = t // (HALF // LT), t % (HALF // LT)
            v = lab[i, r * LT:(r + 1) * LT, :]
            inner = lax.dot_general(v, src[...], (((1,), (1,)), ((), ())), preferred_element_type=F32)
            parts = []
            for c in range(n // 128):
                part = h - inner[:, c * 128:(c + 1) * 128]
                parts.append(jnp.min(part.reshape(LT // 8, 8, 128), axis=0))
            best = jnp.minimum(best, jnp.concatenate(parts, axis=1))
        best = jnp.min(best, axis=0, keepdims=True)
        s, row = slot
        for c in range(n // 128):
            res[s, pl.ds(row + c, 1), :] = best[:, c * 128:(c + 1) * 128]

    def own(j):
        task(u.at[pl.ds(pl.multiple_of(k * HALF + j * COLS, COLS), COLS)], (2, 2 * j))

    def got_t1(s, role):
        task(recv.at[s, pl.ds(pl.multiple_of(role * T1, T1), T1)], (s, 2 * role))

    def got_t2(s):
        task(recv.at[s, pl.ds(2 * T1, COLS)], (s, 4))

    def got_c(s):
        task(recv.at[s, pl.ds(2 * T1 + 2 * T2, COLS)], (s, 6))

    def result(s):
        return [
            remote(res.at[s], got.at[s, yl, k], rs.at[s, i], rr.at[s, g], to)
            for i, to in enumerate(groups[s])
        ]

    def result_in(s, i):
        ref = got.at[s, i // 2, i % 2]
        return remote(ref, ref, rs.at[s, i], rr.at[s, i], groups[s][i])

    def share(i, to):
        return remote(kept, near.at[i], fs.at[i], fr.at[i], to)

    def own_squares():
        def step(i, c):
            w = u[pl.ds(pl.multiple_of(k * HALF + i * 128, 128), 128), :].astype(F32)
            w = w * w
            t = w[:, 0:128]
            for c_ in range(1, D // 128):
                t = t + w[:, c_ * 128:(c_ + 1) * 128]
            kept[1, pl.ds(i, 1), :] = jnp.sum(t.T, axis=0, keepdims=True)
            return c
        lax.fori_loop(0, HALF // 128, step, 0)

    def first_half_squares():
        load_l.wait()
        half_squares(0)

    def on_px(i):
        for d in (1, 2, 3):
            pick_x(d).wait_recv()
        ps[0] = pc[x] + pr[0] + pr[1] + pr[2]
        go(pick_y())

    def on_py(i):
        pick_y().wait_recv()
        ps[1] = ps[0] + py[...]
        for d in (1, 2, 3):
            go(pick_z(d))

    def on_pz(i):
        for d in (1, 2, 3):
            pick_z(d).wait_recv()
        pp[x] = ps[1] + pz[0] + pz[1] + pz[2]
        for d in (1, 2, 3):
            go(pick_g(d))

    def on_pg(i):
        for d in (1, 2, 3):
            pick_g_in(d).wait_recv()
        go(pick_c())

    def pick_squares():
        for j in range(4):
            pmat[0:PK, j * 256:(j + 1) * 256] = pp[j]
            pmat[PK:2 * PK, j * 256:(j + 1) * 256] = pq[j]
        w = pmat[...].astype(F32)
        psq[...] = jnp.broadcast_to(0.5 * jnp.sum(w * w, axis=1, keepdims=True), (2 * PK, 128))

    def pick_tasks():
        for j in range(HALF // COLS):
            v = u[pl.ds(pl.multiple_of(k * HALF + j * COLS, COLS), COLS), :]
            inner = lax.dot_general(pmat[...], v, (((1,), (1,)), ((), ())), preferred_element_type=F32)
            for c in range(COLS // 128):
                part = jnp.min(psq[...] - inner[:, c * 128:(c + 1) * 128], axis=0, keepdims=True)
                row = 2 * j + c
                res[2, row:row + 1, :] = jnp.minimum(res[2, row:row + 1, :], part)

    events = {
        "m1": on_m1, "m2": on_m2, "p1": on_p1, "p2": on_p2, "p3": on_p3,
        "y0": lambda i: across_in(0, i).wait_recv(), "y1": lambda i: across_in(1, i).wait_recv(),
        "L": lambda i: swap_l.wait_recv(),
        "px": on_px, "py": on_py, "pz": on_pz, "pg": on_pg, "pc": lambda i: pick_c().wait_recv(),
    }
    work = {
        "gather": gather_picks, "hsq0": first_half_squares, "hsq1": lambda: half_squares(1),
        "usq": own_squares, "psq": pick_squares, "ptask": pick_tasks,
        "own0": lambda: own(0), "own1": lambda: own(1), "own2": lambda: own(2), "own3": lambda: own(3),
        "A0": lambda: got_t1(0, role1), "A1": lambda: got_t1(1, role2),
        "B0": lambda: got_t1(0, 1 - role1), "B1": lambda: got_t1(1, 1 - role2),
        "E0": lambda: got_t2(0), "E1": lambda: got_t2(1), "F0": lambda: got_c(0), "F1": lambda: got_c(1),
    }
    finished = [0, 0]
    for step in ORDER:
        if len(step) == 2:
            events[step[0]](step[1])
        else:
            work[step[0]]()
            if step[0] == "ptask":
                kept[0] = res[2]
                for i, to in enumerate((core, yside, ydiag)):
                    go(share(i, to))
            if step[0][0] in "ABEF":
                s = int(step[0][1])
                finished[s] += 1
                if finished[s] == 4:
                    for copy in result(s):
                        go(copy)

    for i, to in enumerate((core, yside, ydiag)):
        share(i, to).wait_recv()
    here = jnp.minimum(kept[0], near[1, 0])
    there = jnp.minimum(near[0, 0], near[2, 0])
    for s in (1, 0):
        for i in range(4):
            result_in(s, i).wait_recv()
        here = jnp.minimum(here, jnp.minimum(got[s, 0, k], got[s, 1, k]))
        there = jnp.minimum(there, jnp.minimum(got[s, 0, 1 - k], got[s, 1, 1 - k]))
    out_ref[k] = (kept[1] + 2.0 * here) * (1.0 / D)
    out_ref[1 - k] = (near[0, 1] + 2.0 * there) * (1.0 / D)
    for copy in started:
        copy.wait_send()


def body(unlabeled, labeled, picks):
    n_rows = unlabeled.shape[0]
    dma = pltpu.SemaphoreType.DMA
    vm = pltpu.VMEM
    out = pl.pallas_call(
        kernel,
        out_shape=jax.ShapeDtypeStruct((2, 8, 128), F32),
        in_specs=[
            pl.BlockSpec(memory_space=pl.ANY),
            pl.BlockSpec(memory_space=pl.ANY),
            pl.BlockSpec(memory_space=pltpu.VMEM),
        ],
        out_specs=pl.BlockSpec(memory_space=pltpu.VMEM),
        scratch_shapes=[
            vm((n_rows, D), BF16), vm((2, HALF, D), BF16), vm((2 * HALF, 128), F32),
            vm((2, HALF, D), BF16), vm((NP * Q, D), BF16), vm((128, 128), jnp.int32),
            vm((4, PK, 256), BF16), vm((3, PK, 256), BF16), vm((2, PK, 256), BF16),
            vm((PK, 256), BF16), vm((3, PK, 256), BF16), vm((4, PK, 256), BF16),
            vm((4, PK, 256), BF16), vm((2 * PK, D), BF16), vm((2 * PK, 128), F32),
            vm((3, 8, 128), F32), vm((2, 2, 2, 8, 128), F32), vm((2, 8, 128), F32), vm((3, 2, 8, 128), F32),
            dma((2,)), dma((2,)), dma((NM,)), dma((NM,)), dma((NM,)), dma((NM,)),
            dma((NP,)), dma((NP,)), dma((NP,)), dma((NP,)), dma((NP,)), dma((NP,)),
            dma((2, NT1 + NT2)), dma((2, NT1 + NT2)),
            dma((7,)), dma((7,)), dma((4,)), dma((4,)), dma((2, 4)), dma((2, 4)), dma((3,)), dma((3,)),
        ],
        compiler_params=pltpu.CompilerParams(
            collective_id=0, has_side_effects=True, vmem_limit_bytes=60 << 20
        ),
    )(unlabeled, labeled, picks.reshape(1, -1))
    return out.reshape(-1)


def solution(mesh):
    return jax.shard_map(
        body,
        mesh=mesh,
        in_specs=(P("blk", None), P(("grp", "blk"), None), P()),
        out_specs=P("blk"),
        check_vma=False,
    )
```
